32 devices in a mesh: cuts: 2 (over x), frame: 8 (over z, y), coil: 2 (over core).
Axes of the slice: x: 2, y: 2, z: 4, core: 2. Of those that a mesh axis runs over, the one named last changes fastest.
Arguments:
- spatial: bfloat16 [512, 32, 512], P(('cuts', 'coil', 'frame')), parts along dimension 0, may hold values from -6 to 6
- temporal: bfloat16 [32, 64], P(('cuts', 'frame')), parts along dimension 0, may hold values from -0.75 to 0.75
- kspace: bfloat16 [32, 32, 256, 512], P(('cuts', 'frame'), 'coil'), parts along dimension 0, may hold values from -2 to 2
- sampled: int32 [32, 256], P(('cuts', 'frame')), parts along dimension 0, may hold values 0 or 1
- sensitivity: bfloat16 [64, 256, 512], P(('cuts', 'coil')), parts along dimension 0, may hold values from -1 to 1
Outputs:
- spatial_grad: float32 [512, 32, 512], P(('cuts', 'coil', 'frame')), parts along dimension 0
- temporal_grad: float32 [32, 64], P(('cuts', 'frame')), parts along dimension 0
The draws below stay inside these ranges and needn't reach their ends.
There are 2 independent parts, one for each index of `cuts`. The reference program is written for one: setup_inputs(seed, part) draws one part's arguments, and reference() takes and returns one part's arrays. A program takes and returns all parts, laid end to end along the dimension named above; each array names one. Nothing has to cross between parts.
All inputs are finite; a program needn't handle non-finite values. No bound on the sum of `sampled` on one device may be relied on, other than what follows from the above.
Results may differ from the reference program's by a relative error of at most 0.003.
Values may be sent and summed in bfloat16 or wider, within the bound.
A program may use at most 128 MiB of HBM per device.

```python
import math
import jax
import jax.numpy as jnp
from jax import lax

NX = 256
NY = 256
RANK = 32
COILS = 32
FRAMES = 16


def plant(array, own_key, least, high):
    extent = array.shape
    place = [jax.random.randint(jax.random.fold_in(own_key, axis), (), 0, extent[axis]) for axis in range(len(extent))]
    array = array.at[tuple(place)].set(least)
    longest = extent.index(max(extent))
    place[longest] = (place[longest] + 1) % extent[longest]
    return array.at[tuple(place)].set(high)


def steps_of(rng, extent, shards, low, largest):
    level = 1.0
    for axis_at, shards_of in shards:
        draws = jax.random.uniform(jax.random.fold_in(jax.random.fold_in(rng, 6), axis_at), (shards_of,), jnp.float32, low / len(shards), largest / len(shards))
        level = level * jnp.repeat(jnp.exp(draws), extent[axis_at] // shards_of).reshape((-1,) + (1,) * (len(extent) - 1 - axis_at))
    return level


def centred(own_key, extent, spread, bound, pieces=(), held_as=jnp.bfloat16):
    gain = steps_of(own_key, extent, pieces, -0.22, 0.18) if pieces else 1.0
    values = jax.random.normal(own_key, extent, jnp.float32) * spread * gain
    return jnp.minimum(jnp.maximum(values, -bound), bound).astype(held_as)


def setup_inputs(seed: int = 0, part: int = 0) -> dict:
    seeds = jax.random.split(jax.random.key(seed), 6)
    part_splits = jax.random.split(jax.random.fold_in(seeds[5], part), 6)
    spatial = centred(part_splits[0], (NX, RANK, 2 * NY), 1.0, 6.0, ((0, 16),))
    temporal = centred(part_splits[1], (FRAMES, 2 * RANK), (2 * RANK) ** -0.5, 0.75, ((0, 8),))
    kspace = centred(part_splits[2], (FRAMES, COILS, NX, 2 * NY), 0.3, 2.0, ((0, 8), (1, 2)))
    sampled = plant((jax.random.randint(part_splits[3], (FRAMES, NY), 0, 3) < 1).astype(jnp.int32), jax.random.fold_in(part_splits[3], 1), 0, 1)
    sensitivity = centred(part_splits[4], (COILS, NX, 2 * NY), 0.18, 1.0, ((0, 2),))
    return {"spatial": spatial, "temporal": temporal, "kspace": kspace, "sampled": sampled, "sensitivity": sensitivity}


def split_parts(values):
    half_width = values.shape[-1] // 2
    return (values[..., :half_width], values[..., half_width:])

def dft_block(length):
    index = jnp.arange(length, dtype=jnp.int32)
    angles = (index[:, None] * index[None, :] % length).astype(jnp.float32) * (2.0 * math.pi / length)
    norm_factor = 1.0 / math.sqrt(length)
    cosine = jnp.cos(angles) * norm_factor
    sine_part = -jnp.sin(angles) * norm_factor
    upper_rows = jnp.concatenate([cosine, sine_part], 1)
    lower_rows = jnp.concatenate([-sine_part, cosine], 1)
    return jnp.concatenate([upper_rows, lower_rows], 0).astype(jnp.bfloat16)

def coil_adjoint(image, measured, sampled_row, sensitivity, block):
    image_real, image_imag = split_parts(image.astype(jnp.float32))
    sens_real, sens_imag = split_parts(sensitivity.astype(jnp.float32))
    coil_real = sens_real * image_real[None] - sens_imag * image_imag[None]
    coil_imag = sens_real * image_imag[None] + sens_imag * image_real[None]
    coil_image = jnp.concatenate([coil_real, coil_imag], -1).astype(jnp.bfloat16)
    coil_count, row_count, full_width = coil_image.shape
    spectrum = jnp.dot(coil_image.reshape(coil_count * row_count, full_width), block, preferred_element_type=jnp.float32).reshape(coil_count, row_count, full_width)
    line_keep = jnp.concatenate([sampled_row, sampled_row]).astype(jnp.float32)
    misfit = (line_keep * (spectrum - measured.astype(jnp.float32))).astype(jnp.bfloat16)
    adjoint = jnp.dot(misfit.reshape(coil_count * row_count, full_width), block.T, preferred_element_type=jnp.float32).reshape(coil_count, row_count, full_width)
    back_real, back_imag = split_parts(adjoint)
    grad_real = lax.optimization_barrier(jnp.sum(sens_real * back_real + sens_imag * back_imag, axis=0))
    grad_imag = lax.optimization_barrier(jnp.sum(sens_real * back_imag - sens_imag * back_real, axis=0))
    return jnp.concatenate([grad_real, grad_imag], -1)

def reference(spatial, temporal, kspace, sampled, sensitivity):
    spat = spatial.astype(jnp.float32)
    temp = temporal.astype(jnp.float32)
    spat_real, spat_imag = split_parts(spat)
    temp_real, temp_imag = split_parts(temp)
    image_real = jnp.einsum('tr,xry->txy', temp_real, spat_real) - jnp.einsum('tr,xry->txy', temp_imag, spat_imag)
    image_imag = jnp.einsum('tr,xry->txy', temp_real, spat_imag) + jnp.einsum('tr,xry->txy', temp_imag, spat_real)
    image = jnp.concatenate([image_real, image_imag], -1).astype(jnp.bfloat16)
    block = dft_block(spatial.shape[2] // 2)
    grads = lax.map(lambda frame_item: coil_adjoint(frame_item[0], frame_item[1], frame_item[2], sensitivity, block), (image, kspace, sampled))
    grad_image = grads.astype(jnp.bfloat16).astype(jnp.float32)
    grad_real, grad_imag = split_parts(grad_image)
    spatial_real = jnp.einsum('tr,txy->xry', temp_real, grad_real) + jnp.einsum('tr,txy->xry', temp_imag, grad_imag)
    spatial_imag = jnp.einsum('tr,txy->xry', temp_real, grad_imag) - jnp.einsum('tr,txy->xry', temp_imag, grad_real)
    spatial_grad = jnp.concatenate([spatial_real, spatial_imag], -1)
    temporal_real = jnp.einsum('xry,txy->tr', spat_real, grad_real) + jnp.einsum('xry,txy->tr', spat_imag, grad_imag)
    temporal_imag = jnp.einsum('xry,txy->tr', spat_real, grad_imag) - jnp.einsum('xry,txy->tr', spat_imag, grad_real)
    temporal_grad = jnp.concatenate([temporal_real, temporal_imag], -1)
    return (spatial_grad, temporal_grad)
```

```python
import functools
import math

import jax
import jax.numpy as jnp
import ml_dtypes
import numpy as np
from jax import lax
from jax.experimental import pallas as pl
from jax.experimental.pallas import tpu as pltpu
from jax.sharding import PartitionSpec as P

BF = jnp.bfloat16
F32 = jnp.float32
MESH = pl.DeviceIdType.MESH
ROW_TILE = 16
LANES = 128


def dft_block(length):
    index = np.arange(length, dtype=np.int64)
    angles = (index[:, None] * index[None, :] % length) * (2.0 * math.pi / length)
    norm_factor = 1.0 / math.sqrt(length)
    cosine = np.cos(angles) * norm_factor
    sine_part = -np.sin(angles) * norm_factor
    block = np.block([[cosine, sine_part], [-sine_part, cosine]])
    return block.astype(np.float32).astype(ml_dtypes.bfloat16)


def mm(a, b):
    return jnp.dot(a, b, preferred_element_type=F32)


def mm_nt(a, b):
    return lax.dot_general(a, b, (((1,), (1,)), ((), ())), preferred_element_type=F32)


def xor(a, b, count):
    if count & (count - 1):
        return lax.rem(a + b, count)
    total, bit = 0, 1
    while bit < count:
        total = total + bit * lax.rem(a // bit + b // bit, 2)
        bit *= 2
    return total


def iota(shape, dim):
    return lax.broadcasted_iota(jnp.int32, shape, dim)


def one_hot(condition):
    return jnp.where(condition, 1.0, 0.0).astype(BF)


def kernel(
    dims,
    spatial_hbm, temporal_ref, kspace_hbm, sampled_ref, sens_hbm, block_hbm,
    out_hbm, tgrad_ref,
    kbuf, sbuf, spat, block, back, tslot, tall, img_send, img_recv, img_f32,
    at_real, at_imag, part_own, part_out, part_in, g_send, g_recv, g_full,
    outv, tg_send, tg_recv,
    k_sem, s_sem, spat_sem, block_sem, out_sem,
    t_ssem, t_rsem, i_ssem, i_rsem, f_ssem, f_rsem, p_ssem, p_rsem,
    g_ssem, g_rsem, tg_ssem, tg_rsem,
):
    nf, nc, frames, coils, rows, rank, width, chunk, pieces, chunks = dims
    half = width // 2
    total_frames = nf * frames
    f, c = lax.axis_index("frame"), lax.axis_index("coil")
    other = nc - 1 - c
    mine = f // pieces

    def order(step):
        if chunks < 3:
            return step
        later = (step + chunks - 1) // chunks
        return (lax.rem(step, chunks - 1) + 1) * later

    def chunk_at(step):
        return xor(mine, order(step), chunks)

    def remote(src, dst, ssem, rsem, frame, coil):
        return pltpu.make_async_remote_copy(
            src_ref=src, dst_ref=dst, send_sem=ssem, recv_sem=rsem,
            device_id={"frame": frame, "coil": coil}, device_id_type=MESH,
        )

    spat_copy = pltpu.make_async_copy(spatial_hbm, spat, spat_sem)
    block_copy = pltpu.make_async_copy(block_hbm, block, block_sem)

    def chunk_copies(step, part):
        owner = c if part == 0 else other
        start = pl.multiple_of((owner * chunks + chunk_at(step)) * chunk, chunk)
        window = pl.ds(start, chunk)
        return (
            pltpu.make_async_copy(
                kspace_hbm.at[:, :, window, :], kbuf.at[part, step], k_sem.at[part, step]
            ),
            pltpu.make_async_copy(
                sens_hbm.at[:, window, :], sbuf.at[part, step], s_sem.at[part, step]
            ),
        )

    block_copy.start()
    spat_copy.start()

    barrier = pltpu.get_barrier_semaphore()
    for shift in range(nf):
        for coil in range(nc):
            if shift or coil:
                pl.semaphore_signal(
                    barrier, inc=1,
                    device_id={"frame": xor(f, shift, nf), "coil": lax.rem(c + coil, nc)},
                    device_id_type=MESH,
                )

    @pl.loop(0, chunks)
    def _(step):
        for part in range(nc):
            for copy in chunk_copies(step, part):
                copy.start()

    tslot[f] = jnp.concatenate(
        [
            temporal_ref[...].astype(F32),
            jnp.zeros((frames, LANES - 2 * rank), F32),
        ],
        -1,
    )

    pl.semaphore_wait(barrier, nf * nc - 1)
    for shift in range(1, nf):
        to = xor(f, shift, nf)
        remote(tslot.at[f], tslot.at[f], t_ssem.at[to], t_rsem.at[f], to, c).start()

    block_copy.wait()
    cosine, sine = block[:half, :half], block[:half, half:]
    transposed = jnp.concatenate(
        [jnp.concatenate([cosine, -sine], 1), jnp.concatenate([sine, cosine], 1)], 0
    )
    diagonal = iota((width, width), 0) == iota((width, width), 1)
    for t in range(frames):
        keep = sampled_ref[t : t + 1, :].astype(F32)
        keep = jnp.concatenate([keep, keep], -1)
        selector = jnp.where(diagonal, keep, 0.0).astype(BF)
        back[t] = mm(selector, transposed).astype(BF)

    spat_copy.wait()
    for shift in range(1, nf):
        source = xor(f, shift, nf)
        remote(
            tslot.at[source], tslot.at[source], t_ssem.at[source], t_rsem.at[source], source, c
        ).wait_recv()
    for source in range(nf):
        tall[source * frames : (source + 1) * frames] = tslot[source]
    long, deep = total_frames * rows, rows * rank
    repeat = one_hot(iota((long, total_frames), 0) // rows == iota((long, total_frames), 1))
    repeated = mm(repeat, tall[...].astype(BF)).astype(BF)
    lane, column = iota((LANES, deep), 0), iota((LANES, deep), 1)
    same_row = lax.rem(iota((long, deep), 0), rows) == iota((long, deep), 1) // rank
    spread_real = one_hot(lane == lax.rem(column, rank))
    spread_imag = one_hot(lane == lax.rem(column, rank) + rank)
    a_real = jnp.where(same_row, mm(repeated, spread_real), 0.0).astype(BF)
    a_imag = jnp.where(same_row, mm(repeated, spread_imag), 0.0).astype(BF)
    factors = spat[...].reshape(deep, width)
    by_real, by_imag = mm(a_real, factors), mm(a_imag, factors)
    image = jnp.concatenate(
        [by_real[:, :half] - by_imag[:, half:], by_real[:, half:] + by_imag[:, :half]], -1
    )
    for to in range(nf):
        for t in range(frames):
            at = (to * frames + t) * rows
            img_send[to, t] = image[at : at + rows].astype(BF)
    img_recv[0, f] = img_send[f]
    for shift in range(1, nf):
        shift = shift if nf < 3 else shift % (nf - 1) + 1
        to = xor(f, shift, nf)
        remote(
            img_send.at[to], img_recv.at[0, f], i_ssem.at[to], i_rsem.at[f], to, c
        ).start()

    row, lane = iota((deep, LANES), 0), iota((deep, LANES), 1)
    same_column = iota((deep, long), 0) // rank == lax.rem(iota((deep, long), 1), rows)
    from_real = one_hot(lane == lax.rem(row, rank))
    from_imag = one_hot(lane == lax.rem(row, rank) + rank)
    at_real[...] = jnp.where(same_column, mm_nt(from_real, repeated), 0.0).astype(BF)
    at_imag[...] = jnp.where(same_column, mm_nt(from_imag, repeated), 0.0).astype(BF)

    def image_copy(source):
        return remote(
            img_send.at[source], img_recv.at[0, source], i_ssem.at[source], i_rsem.at[source],
            source, c,
        )

    def forward_copy(source):
        return remote(
            img_recv.at[0, source], img_recv.at[1, source], f_ssem.at[source],
            f_rsem.at[source], f, other,
        )

    def partial_copy(step):
        return remote(
            part_out.at[step], part_in.at[step], p_ssem.at[step], p_rsem.at[step], f, other
        )

    def gradient(step, part):
        where = chunk_at(step)
        for i in range(pieces):
            for t in range(frames):
                img_f32[t, i * rows : (i + 1) * rows] = img_recv[
                    part, where * pieces + i, t
                ].astype(F32)
        for copy in chunk_copies(step, part):
            copy.wait()
        sums = []
        for t in range(frames):
            image_real, image_imag = img_f32[t, :, :half], img_f32[t, :, half:]
            sens = sbuf[part, step].astype(F32)
            sens_real, sens_imag = sens[..., :half], sens[..., half:]
            coil_image = jnp.concatenate(
                [
                    sens_real * image_real[None] - sens_imag * image_imag[None],
                    sens_real * image_imag[None] + sens_imag * image_real[None],
                ],
                -1,
            ).astype(BF)
            spectrum = mm(coil_image.reshape(coils * chunk, width), block[...])
            measured = kbuf[part, step, t].reshape(coils * chunk, width).astype(F32)
            misfit = (spectrum - measured).astype(BF)
            adjoint = mm(misfit, back[t]).reshape(coils, chunk, width)
            back_real, back_imag = adjoint[..., :half], adjoint[..., half:]
            sums.append(
                jnp.concatenate(
                    [
                        jnp.sum(sens_real * back_real + sens_imag * back_imag, axis=0),
                        jnp.sum(sens_real * back_imag - sens_imag * back_real, axis=0),
                    ],
                    -1,
                )
            )
        return sums

    def finish(step):
        where = chunk_at(step)
        partial_copy(step).wait_recv()
        for t in range(frames):
            total = part_own[step, t] + part_in[step, t]
            for i in range(pieces):
                g_send[where * pieces + i, t] = total[i * rows : (i + 1) * rows].astype(BF)
        for i in range(pieces):
            to = where * pieces + i

            @pl.when(to != f)
            def _():
                remote(
                    g_send.at[to], g_recv.at[f], g_ssem.at[to], g_rsem.at[f], to, c
                ).start()

            @pl.when(to == f)
            def _():
                g_recv[f] = g_send[f]

    @pl.loop(0, chunks)
    def _(step):
        where = chunk_at(step)
        for i in range(pieces):
            source = where * pieces + i

            @pl.when(source != f)
            def _():
                image_copy(source).wait_recv()

            forward_copy(source).start()
        for t, value in enumerate(gradient(step, 0)):
            part_own[step, t] = value

        @pl.when(step > 0)
        def _():
            finish(step - 1)

        for i in range(pieces):
            forward_copy(where * pieces + i).wait_recv()
        for t, value in enumerate(gradient(step, 1)):
            part_out[step, t] = value
        partial_copy(step).start()

    finish(chunks - 1)

    def gradient_copy(source):
        return remote(
            g_send.at[source], g_recv.at[source], g_ssem.at[source], g_rsem.at[source], source, c
        )

    for shift in range(1, nf):
        gradient_copy(xor(f, shift, nf)).wait_recv()
    for source in range(nf):
        for t in range(frames):
            at = (source * frames + t) * rows
            g_full[at : at + rows] = g_recv[source, t].astype(F32)
    grad = g_full[...].astype(BF)
    turned = jnp.concatenate([grad[:, half:], -grad[:, :half]], -1)
    factors = spat[...].reshape(deep, width)
    fold_row, fold_lane = iota((deep, LANES), 0), iota((deep, LANES), 1)
    pooled = jnp.zeros((long, LANES), F32)
    for values, shift in ((grad, 0), (turned, rank)):
        products = jnp.where(same_row, mm_nt(values, factors), 0.0)
        fold = one_hot(lax.rem(fold_row, rank) + shift == fold_lane)
        high = products.astype(BF)
        low = (products - high.astype(F32)).astype(BF)
        pooled = pooled + mm(high, fold) + mm(low, fold)
    gather = one_hot(iota((total_frames, long), 0) == iota((total_frames, long), 1) // rows)
    high = pooled.astype(BF)
    low = (pooled - high.astype(F32)).astype(BF)
    temporal_part = mm(gather, high) + mm(gather, low)
    for to in range(nf):
        tg_send[to] = temporal_part[to * frames : (to + 1) * frames]
    tg_recv[c, f] = tg_send[f]
    for shift in range(nf):
        for coil in range(nc):
            if shift or coil:
                to, at = xor(f, shift, nf), lax.rem(c + coil, nc)
                remote(
                    tg_send.at[to], tg_recv.at[c, f], tg_ssem.at[at, to], tg_rsem.at[c, f], to, at
                ).start()

    by_real, by_imag = mm(at_real[...], grad), mm(at_imag[...], grad)
    outv[...] = jnp.concatenate(
        [by_real[:, :half] + by_imag[:, half:], by_real[:, half:] - by_imag[:, :half]], -1
    ).reshape(rows, rank, width)
    out_copy = pltpu.make_async_copy(outv, out_hbm, out_sem)
    out_copy.start()

    for shift in range(nf):
        for coil in range(nc):
            if shift or coil:
                to, at = xor(f, shift, nf), lax.rem(c + coil, nc)
                remote(
                    tg_send.at[to], tg_recv.at[at, to], tg_ssem.at[at, to], tg_rsem.at[at, to],
                    to, at,
                ).wait()
    summed = tg_recv[0, 0]
    for coil in range(nc):
        for source in range(nf):
            if coil or source:
                summed = summed + tg_recv[coil, source]
    tgrad_ref[...] = summed[:, : 2 * rank]

    for shift in range(nf):
        to = xor(f, shift, nf)
        forward_copy(to).wait_send()
        if shift:
            remote(tslot.at[f], tslot.at[f], t_ssem.at[to], t_rsem.at[f], to, c).wait_send()
            image_copy(to).wait_send()
            gradient_copy(to).wait_send()

    @pl.loop(0, chunks)
    def _(step):
        partial_copy(step).wait_send()

    out_copy.wait()


def on_device(nf, nc, spatial, temporal, kspace, sampled, sensitivity):
    rows, rank, width = spatial.shape
    frames, coils = kspace.shape[:2]
    chunk = max(rows, ROW_TILE)
    pieces = chunk // rows
    chunks = nf // pieces
    total_frames = nf * frames
    long, deep = total_frames * rows, rows * rank
    dims = (nf, nc, frames, coils, rows, rank, width, chunk, pieces, chunks)
    vmem, dma = pltpu.VMEM, pltpu.SemaphoreType.DMA
    anywhere, inside = pl.BlockSpec(memory_space=pl.ANY), pl.BlockSpec(memory_space=pltpu.VMEM)
    return pl.pallas_call(
        functools.partial(kernel, dims),
        out_shape=(
            jax.ShapeDtypeStruct(spatial.shape, F32),
            jax.ShapeDtypeStruct(temporal.shape, F32),
        ),
        in_specs=[anywhere, inside, anywhere, inside, anywhere, anywhere],
        out_specs=(anywhere, inside),
        scratch_shapes=[
            vmem((nc, chunks, frames, coils, chunk, width), BF),
            vmem((nc, chunks, coils, chunk, width), BF),
            vmem((rows, rank, width), BF),
            vmem((width, width), BF),
            vmem((frames, width, width), BF),
            vmem((nf, frames, LANES), F32),
            vmem((total_frames, LANES), F32),
            vmem((nf, frames, rows, width), BF),
            vmem((nc, nf, frames, rows, width), BF),
            vmem((frames, chunk, width), F32),
            vmem((deep, long), BF),
            vmem((deep, long), BF),
            vmem((chunks, frames, chunk, width), F32),
            vmem((chunks, frames, chunk, width), F32),
            vmem((chunks, frames, chunk, width), F32),
            vmem((nf, frames, rows, width), BF),
            vmem((nf, frames, rows, width), BF),
            vmem((long, width), F32),
            vmem((rows, rank, width), F32),
            vmem((nf, frames, LANES), F32),
            vmem((nc, nf, frames, LANES), F32),
            dma((nc, chunks)),
            dma((nc, chunks)),
            dma,
            dma,
            dma,
        ]
        + [dma((nf,))] * 6
        + [dma((chunks,))] * 2
        + [dma((nf,))] * 2
        + [dma((nc, nf))] * 2,
        compiler_params=pltpu.CompilerParams(
            collective_id=0, has_side_effects=True, vmem_limit_bytes=56 * 1024 * 1024
        ),
        cost_estimate=pl.CostEstimate(
            flops=8 * frames * coils * nc * chunks * chunk * width * width // 2,
            bytes_accessed=kspace.size * 2 + sensitivity.size * 2 + spatial.size * 6,
            transcendentals=0,
        ),
    )(spatial, temporal, kspace, sampled, sensitivity, jnp.asarray(dft_block(width // 2)))


def solution(mesh):
    placed = (
        P(("cuts", "coil", "frame"), None, None),
        P(("cuts", "frame"), None),
        P(("cuts", "frame"), "coil", None, None),
        P(("cuts", "frame"), None),
        P(("cuts", "coil"), None, None),
    )
    return jax.shard_map(
        functools.partial(on_device, mesh.shape["frame"], mesh.shape["coil"]),
        mesh=mesh,
        in_specs=placed,
        out_specs=(P(("cuts", "coil", "frame"), None, None), P(("cuts", "frame"), None)),
        check_vma=False,
    )
```

```python
import functools
import math

import jax
import jax.numpy as jnp
import ml_dtypes
import numpy as np
from jax import lax
from jax.experimental import pallas as pl
from jax.experimental.pallas import tpu as pltpu
from jax.sharding import PartitionSpec as P

BF = jnp.bfloat16
F32 = jnp.float32
MESH = pl.DeviceIdType.MESH
ROW_TILE = 16
LANES = 128


def dft_block(length):
    index = np.arange(length, dtype=np.int64)
    angles = (index[:, None] * index[None, :] % length) * (2.0 * math.pi / length)
    norm_factor = 1.0 / math.sqrt(length)
    cosine = np.cos(angles) * norm_factor
    sine_part = -np.sin(angles) * norm_factor
    block = np.block([[cosine, sine_part], [-sine_part, cosine]])
    return block.astype(np.float32).astype(ml_dtypes.bfloat16)


def mm(a, b):
    return jnp.dot(a, b, preferred_element_type=F32)


def mm_nt(a, b):
    return lax.dot_general(a, b, (((1,), (1,)), ((), ())), preferred_element_type=F32)


def xor(a, b, count):
    if count & (count - 1):
        return lax.rem(a + b, count)
    total, bit = 0, 1
    while bit < count:
        total = total + bit * lax.rem(a // bit + b // bit, 2)
        bit *= 2
    return total


def iota(shape, dim):
    return lax.broadcasted_iota(jnp.int32, shape, dim)


def one_hot(condition):
    return jnp.where(condition, 1.0, 0.0).astype(BF)


def kernel(
    dims,
    spatial_hbm, temporal_ref, kspace_hbm, sampled_ref, sens_hbm, block_hbm,
    out_hbm, tgrad_ref,
    kbuf, sbuf, spat, block, back, keep, ci0, ci1, mis0, mis1, tslot, tall, img_send, img_recv, img_f32,
    at_real, at_imag, part_own, part_out, part_in, g_send, g_recv, g_full,
    outv, tg_send, tg_recv,
    k_sem, s_sem, spat_sem, block_sem, out_sem,
    t_ssem, t_rsem, i_ssem, i_rsem, f_ssem, f_rsem, p_ssem, p_rsem,
    g_ssem, g_rsem, tg_ssem, tg_rsem,
):
    nf, nc, frames, coils, rows, rank, width, chunk, pieces, chunks = dims
    half = width // 2
    total_frames = nf * frames
    f, c = lax.axis_index("frame"), lax.axis_index("coil")
    other = nc - 1 - c
    mine = f // pieces

    def order(step):
        if chunks < 3:
            return step
        later = (step + chunks - 1) // chunks
        return (lax.rem(step, chunks - 1) + 1) * later

    def chunk_at(step):
        return xor(mine, order(step), chunks)

    def remote(src, dst, ssem, rsem, frame, coil):
        return pltpu.make_async_remote_copy(
            src_ref=src, dst_ref=dst, send_sem=ssem, recv_sem=rsem,
            device_id={"frame": frame, "coil": coil}, device_id_type=MESH,
        )

    spat_copy = pltpu.make_async_copy(spatial_hbm, spat, spat_sem)
    block_copy = pltpu.make_async_copy(block_hbm, block, block_sem)

    def chunk_copies(step, part):
        owner = c if part == 0 else other
        start = pl.multiple_of((owner * chunks + chunk_at(step)) * chunk, chunk)
        window = pl.ds(start, chunk)
        return (
            pltpu.make_async_copy(
                kspace_hbm.at[:, :, window, :], kbuf.at[part, step], k_sem.at[part, step]
            ),
            pltpu.make_async_copy(
                sens_hbm.at[:, window, :], sbuf.at[part, step], s_sem.at[part, step]
            ),
        )

    block_copy.start()
    spat_copy.start()

    barrier = pltpu.get_barrier_semaphore()
    for shift in range(nf):
        for coil in range(nc):
            if shift or coil:
                pl.semaphore_signal(
                    barrier, inc=1,
                    device_id={"frame": xor(f, shift, nf), "coil": lax.rem(c + coil, nc)},
                    device_id_type=MESH,
                )

    @pl.loop(0, chunks)
    def _(step):
        for part in range(nc):
            for copy in chunk_copies(step, part):
                copy.start()

    tslot[f] = jnp.concatenate(
        [
            temporal_ref[...].astype(F32),
            jnp.zeros((frames, LANES - 2 * rank), F32),
        ],
        -1,
    )

    pl.semaphore_wait(barrier, nf * nc - 1)
    for shift in range(1, nf):
        to = xor(f, shift, nf)
        remote(tslot.at[f], tslot.at[f], t_ssem.at[to], t_rsem.at[f], to, c).start()

    block_copy.wait()
    cosine, sine = block[:half, :half], block[:half, half:]
    back[:half] = jnp.concatenate([cosine, -sine], 1)
    back[half:] = jnp.concatenate([sine, cosine], 1)
    for t in range(frames):
        lines = sampled_ref[t : t + 1, :].astype(F32)
        lines = jnp.concatenate([lines, lines], -1)
        keep[t] = jnp.broadcast_to(lines, (chunk, width)).astype(BF)
    mis1[...] = jnp.zeros_like(mis1)

    spat_copy.wait()
    for shift in range(1, nf):
        source = xor(f, shift, nf)
        remote(
            tslot.at[source], tslot.at[source], t_ssem.at[source], t_rsem.at[source], source, c
        ).wait_recv()
    for source in range(nf):
        tall[source * frames : (source + 1) * frames] = tslot[source]
    long, deep = total_frames * rows, rows * rank
    repeat = one_hot(iota((long, total_frames), 0) // rows == iota((long, total_frames), 1))
    repeated = mm(repeat, tall[...].astype(BF)).astype(BF)
    lane, column = iota((LANES, deep), 0), iota((LANES, deep), 1)
    same_row = lax.rem(iota((long, deep), 0), rows) == iota((long, deep), 1) // rank
    spread_real = one_hot(lane == lax.rem(column, rank))
    spread_imag = one_hot(lane == lax.rem(column, rank) + rank)
    a_real = jnp.where(same_row, mm(repeated, spread_real), 0.0).astype(BF)
    a_imag = jnp.where(same_row, mm(repeated, spread_imag), 0.0).astype(BF)
    factors = spat[...].reshape(deep, width)
    by_real, by_imag = mm(a_real, factors), mm(a_imag, factors)
    image = jnp.concatenate(
        [by_real[:, :half] - by_imag[:, half:], by_real[:, half:] + by_imag[:, :half]], -1
    )
    for to in range(nf):
        for t in range(frames):
            at = (to * frames + t) * rows
            img_send[to, t] = image[at : at + rows].astype(BF)
    img_recv[0, f] = img_send[f]
    for shift in range(1, nf):
        shift = shift if nf < 3 else shift % (nf - 1) + 1
        to = xor(f, shift, nf)
        remote(
            img_send.at[to], img_recv.at[0, f], i_ssem.at[to], i_rsem.at[f], to, c
        ).start()

    row, lane = iota((deep, LANES), 0), iota((deep, LANES), 1)
    same_column = iota((deep, long), 0) // rank == lax.rem(iota((deep, long), 1), rows)
    from_real = one_hot(lane == lax.rem(row, rank))
    from_imag = one_hot(lane == lax.rem(row, rank) + rank)
    at_real[...] = jnp.where(same_column, mm_nt(from_real, repeated), 0.0).astype(BF)
    at_imag[...] = jnp.where(same_column, mm_nt(from_imag, repeated), 0.0).astype(BF)

    def image_copy(source):
        return remote(
            img_send.at[source], img_recv.at[0, source], i_ssem.at[source], i_rsem.at[source],
            source, c,
        )

    def forward_copy(source):
        return remote(
            img_recv.at[0, source], img_recv.at[1, source], f_ssem.at[source],
            f_rsem.at[source], f, other,
        )

    def partial_copy(step):
        return remote(
            part_out.at[step + 1], part_in.at[step], p_ssem.at[step], p_rsem.at[step], f, other
        )

    tile = (frames, coils, chunk, width)

    def await_chunk(step, part):
        for copy in chunk_copies(step, part):
            copy.wait()

    def coil_images(step, part, out):
        where = chunk_at(step)
        sens = sbuf[part, step].astype(F32)
        sens_real, sens_imag = sens[..., :half], sens[..., half:]
        size = coils * chunk
        for t in range(frames):
            if pieces == 1:
                image = img_recv[part, where, t].astype(F32)
            else:
                for i in range(pieces):
                    img_f32[part, t, i * rows : (i + 1) * rows] = img_recv[
                        part, where * pieces + i, t
                    ].astype(F32)
                image = img_f32[part, t]
            image_real, image_imag = image[:, :half], image[:, half:]
            real = sens_real * image_real[None] - sens_imag * image_imag[None]
            imag = sens_real * image_imag[None] + sens_imag * image_real[None]
            out[t * size : (t + 1) * size, :half] = real.astype(BF).reshape(size, half)
            out[t * size : (t + 1) * size, half:] = imag.astype(BF).reshape(size, half)

    def misfits(step, part, source, out):
        spectrum = mm(source[...], block[...]).reshape(tile)
        for t in range(frames):
            misfit = (spectrum[t] - kbuf[part, step, t].astype(F32)).astype(BF) * keep[t][None]
            size = coils * chunk
            out[t * size : (t + 1) * size] = misfit.reshape(size, width)

    def coil_sums(step, part, source, out, slot):
        adjoint = mm(source[...], back[...]).reshape(tile)
        sens = sbuf[part, step].astype(F32)
        sens_real, sens_imag = sens[..., :half], sens[..., half:]
        for t in range(frames):
            back_real, back_imag = adjoint[t, ..., :half], adjoint[t, ..., half:]
            out[slot, t, :, :half] = jnp.sum(sens_real * back_real + sens_imag * back_imag, axis=0)
            out[slot, t, :, half:] = jnp.sum(sens_real * back_imag - sens_imag * back_real, axis=0)

    def finish(step):
        where = chunk_at(step)
        partial_copy(step).wait_recv()
        for t in range(frames):
            total = part_own[step, t] + part_in[step, t]
            for i in range(pieces):
                g_send[where * pieces + i, t] = total[i * rows : (i + 1) * rows].astype(BF)
        for i in range(pieces):
            to = where * pieces + i

            @pl.when(to != f)
            def _():
                remote(
                    g_send.at[to], g_recv.at[f], g_ssem.at[to], g_rsem.at[f], to, c
                ).start()

            @pl.when(to == f)
            def _():
                g_recv[f] = g_send[f]

    def forward(step):
        where = chunk_at(step)
        for i in range(pieces):
            source = where * pieces + i

            @pl.when(source != f)
            def _():
                image_copy(source).wait_recv()

            forward_copy(source).start()

    forward(0)
    await_chunk(0, 0)
    coil_images(0, 0, ci0)

    @pl.loop(0, chunks)
    def _(step):
        where = chunk_at(step)
        before = jnp.maximum(step - 1, 0)
        after = jnp.minimum(step + 1, chunks - 1)
        for i in range(pieces):
            forward_copy(where * pieces + i).wait_recv()
        await_chunk(step, 1)
        coil_sums(before, 1, mis1, part_out, step)
        misfits(step, 0, ci0, mis0)
        coil_images(step, 1, ci1)

        @pl.when(step > 0)
        def _():
            partial_copy(step - 1).start()

        @pl.when(step > 1)
        def _():
            finish(step - 2)

        @pl.when(step < chunks - 1)
        def _():
            forward(step + 1)
            await_chunk(step + 1, 0)

        coil_sums(step, 0, mis0, part_own, step)
        misfits(step, 1, ci1, mis1)
        coil_images(after, 0, ci0)

    coil_sums(chunks - 1, 1, mis1, part_out, chunks)
    partial_copy(chunks - 1).start()
    if chunks > 1:
        finish(chunks - 2)
    finish(chunks - 1)

    def gradient_copy(source):
        return remote(
            g_send.at[source], g_recv.at[source], g_ssem.at[source], g_rsem.at[source], source, c
        )

    for shift in range(1, nf):
        gradient_copy(xor(f, shift, nf)).wait_recv()
    for source in range(nf):
        for t in range(frames):
            at = (source * frames + t) * rows
            g_full[at : at + rows] = g_recv[source, t].astype(F32)
    grad = g_full[...].astype(BF)
    turned = jnp.concatenate([grad[:, half:], -grad[:, :half]], -1)
    factors = spat[...].reshape(deep, width)
    fold_row, fold_lane = iota((deep, LANES), 0), iota((deep, LANES), 1)
    pooled = jnp.zeros((long, LANES), F32)
    for values, shift in ((grad, 0), (turned, rank)):
        products = jnp.where(same_row, mm_nt(values, factors), 0.0)
        fold = one_hot(lax.rem(fold_row, rank) + shift == fold_lane)
        high = products.astype(BF)
        low = (products - high.astype(F32)).astype(BF)
        pooled = pooled + mm(high, fold) + mm(low, fold)
    gather = one_hot(iota((total_frames, long), 0) == iota((total_frames, long), 1) // rows)
    high = pooled.astype(BF)
    low = (pooled - high.astype(F32)).astype(BF)
    temporal_part = mm(gather, high) + mm(gather, low)
    for to in range(nf):
        tg_send[to] = temporal_part[to * frames : (to + 1) * frames]
    tg_recv[c, f] = tg_send[f]
    for shift in range(nf):
        for coil in range(nc):
            if shift or coil:
                to, at = xor(f, shift, nf), lax.rem(c + coil, nc)
                remote(
                    tg_send.at[to], tg_recv.at[c, f], tg_ssem.at[at, to], tg_rsem.at[c, f], to, at
                ).start()

    by_real, by_imag = mm(at_real[...], grad), mm(at_imag[...], grad)
    outv[...] = jnp.concatenate(
        [by_real[:, :half] + by_imag[:, half:], by_real[:, half:] - by_imag[:, :half]], -1
    ).reshape(rows, rank, width)
    out_copy = pltpu.make_async_copy(outv, out_hbm, out_sem)
    out_copy.start()

    for shift in range(nf):
        for coil in range(nc):
            if shift or coil:
                to, at = xor(f, shift, nf), lax.rem(c + coil, nc)
                remote(
                    tg_send.at[to], tg_recv.at[at, to], tg_ssem.at[at, to], tg_rsem.at[at, to],
                    to, at,
                ).wait()
    summed = tg_recv[0, 0]
    for coil in range(nc):
        for source in range(nf):
            if coil or source:
                summed = summed + tg_recv[coil, source]
    tgrad_ref[...] = summed[:, : 2 * rank]

    for shift in range(nf):
        to = xor(f, shift, nf)
        forward_copy(to).wait_send()
        if shift:
            remote(tslot.at[f], tslot.at[f], t_ssem.at[to], t_rsem.at[f], to, c).wait_send()
            image_copy(to).wait_send()
            gradient_copy(to).wait_send()

    @pl.loop(0, chunks)
    def _(step):
        partial_copy(step).wait_send()

    out_copy.wait()


def on_device(nf, nc, spatial, temporal, kspace, sampled, sensitivity):
    rows, rank, width = spatial.shape
    frames, coils = kspace.shape[:2]
    chunk = max(rows, ROW_TILE)
    pieces = chunk // rows
    chunks = nf // pieces
    total_frames = nf * frames
    long, deep = total_frames * rows, rows * rank
    dims = (nf, nc, frames, coils, rows, rank, width, chunk, pieces, chunks)
    vmem, dma = pltpu.VMEM, pltpu.SemaphoreType.DMA
    outside, inside = pl.BlockSpec(memory_space=pl.ANY), pl.BlockSpec(memory_space=pltpu.VMEM)
    return pl.pallas_call(
        functools.partial(kernel, dims),
        out_shape=(
            jax.ShapeDtypeStruct(spatial.shape, F32),
            jax.ShapeDtypeStruct(temporal.shape, F32),
        ),
        in_specs=[outside, inside, outside, inside, outside, outside],
        out_specs=(outside, inside),
        scratch_shapes=[
            vmem((nc, chunks, frames, coils, chunk, width), BF),
            vmem((nc, chunks, coils, chunk, width), BF),
            vmem((rows, rank, width), BF),
            vmem((width, width), BF),
            vmem((width, width), BF),
            vmem((frames, chunk, width), BF),
        ]
        + [vmem((frames * coils * chunk, width), BF)] * 4
        + [
            vmem((nf, frames, LANES), F32),
            vmem((total_frames, LANES), F32),
            vmem((nf, frames, rows, width), BF),
            vmem((nc, nf, frames, rows, width), BF),
            vmem((nc, frames, chunk, width), F32),
            vmem((deep, long), BF),
            vmem((deep, long), BF),
            vmem((chunks, frames, chunk, width), F32),
            vmem((chunks + 1, frames, chunk, width), F32),
            vmem((chunks, frames, chunk, width), F32),
            vmem((nf, frames, rows, width), BF),
            vmem((nf, frames, rows, width), BF),
            vmem((long, width), F32),
            vmem((rows, rank, width), F32),
            vmem((nf, frames, LANES), F32),
            vmem((nc, nf, frames, LANES), F32),
            dma((nc, chunks)),
            dma((nc, chunks)),
            dma,
            dma,
            dma,
        ]
        + [dma((nf,))] * 6
        + [dma((chunks,))] * 2
        + [dma((nf,))] * 2
        + [dma((nc, nf))] * 2,
        compiler_params=pltpu.CompilerParams(
            collective_id=0, has_side_effects=True, vmem_limit_bytes=61 * 1024 * 1024
        ),
        cost_estimate=pl.CostEstimate(
            flops=8 * frames * coils * nc * chunks * chunk * width * width // 2,
            bytes_accessed=kspace.size * 2 + sensitivity.size * 2 + spatial.size * 6,
            transcendentals=0,
        ),
    )(spatial, temporal, kspace, sampled, sensitivity, jnp.asarray(dft_block(width // 2)))


def solution(mesh):
    placed = (
        P(("cuts", "coil", "frame"), None, None),
        P(("cuts", "frame"), None),
        P(("cuts", "frame"), "coil", None, None),
        P(("cuts", "frame"), None),
        P(("cuts", "coil"), None, None),
    )
    return jax.shard_map(
        functools.partial(on_device, mesh.shape["frame"], mesh.shape["coil"]),
        mesh=mesh,
        in_specs=placed,
        out_specs=(P(("cuts", "coil", "frame"), None, None), P(("cuts", "frame"), None)),
        check_vma=False,
    )
```

```python
import functools
import math

import jax
import jax.numpy as jnp
import ml_dtypes
import numpy as np
from jax import lax
from jax.experimental import pallas as pl
from jax.experimental.pallas import tpu as pltpu
from jax.sharding import PartitionSpec as P

BF = jnp.bfloat16
F32 = jnp.float32
MESH = pl.DeviceIdType.MESH
ROW_TILE = 16
AHEAD = 3
LANES = 128


def dft_block(length):
    index = np.arange(length, dtype=np.int64)
    angles = (index[:, None] * index[None, :] % length) * (2.0 * math.pi / length)
    norm_factor = 1.0 / math.sqrt(length)
    cosine = np.cos(angles) * norm_factor
    sine_part = -np.sin(angles) * norm_factor
    block = np.block([[cosine, sine_part], [-sine_part, cosine]])
    return block.astype(np.float32).astype(ml_dtypes.bfloat16)


def mm(a, b):
    return jnp.dot(a, b, preferred_element_type=F32)


def mm_nt(a, b):
    return lax.dot_general(a, b, (((1,), (1,)), ((), ())), preferred_element_type=F32)


def xor(a, b, count):
    if count & (count - 1):
        return lax.rem(a + b, count)
    total, bit = 0, 1
    while bit < count:
        total = total + bit * lax.rem(a // bit + b // bit, 2)
        bit *= 2
    return total


def iota(shape, dim):
    return lax.broadcasted_iota(jnp.int32, shape, dim)


def one_hot(condition):
    return jnp.where(condition, 1.0, 0.0).astype(BF)


def kernel(
    dims,
    spatial_hbm, temporal_ref, kspace_hbm, sampled_ref, sens_hbm, block_hbm,
    turn_hbm, grad_hbm, tgrad_ref,
    kbuf, sbuf, spat, block, back, tslot, tall, img_send, img_recv, img_f32,
    turn, part_own, part_out, part_in, g_send, g_recv, g_full,
    grad_rows, tg_send, tg_recv,
    k_sem, s_sem, spat_sem, block_sem, turn_sem, grad_sem,
    t_ssem, t_rsem, i_ssem, i_rsem, f_ssem, f_rsem, p_ssem, p_rsem,
    g_ssem, g_rsem, tg_ssem, tg_rsem,
):
    nf, nc, frames, coils, rows, rank, width, chunk, pieces, chunks = dims
    half = width // 2
    total_frames = nf * frames
    f, c = lax.axis_index("frame"), lax.axis_index("coil")
    other = nc - 1 - c
    mine = f // pieces

    def order(step):
        if chunks < 3:
            return step
        later = (step + chunks - 1) // chunks
        return (lax.rem(step, chunks - 1) + 1) * later

    def chunk_at(step):
        return xor(mine, order(step), chunks)

    def remote(src, dst, ssem, rsem, frame, coil):
        return pltpu.make_async_remote_copy(
            src_ref=src, dst_ref=dst, send_sem=ssem, recv_sem=rsem,
            device_id={"frame": frame, "coil": coil}, device_id_type=MESH,
        )

    spat_copy = pltpu.make_async_copy(spatial_hbm, spat, spat_sem)
    block_copy = pltpu.make_async_copy(block_hbm, block, block_sem)

    def chunk_copies(step, part):
        owner = c if part == 0 else other
        start = pl.multiple_of((owner * chunks + chunk_at(step)) * chunk, chunk)
        window = pl.ds(start, chunk)
        return (
            pltpu.make_async_copy(
                kspace_hbm.at[:, :, window, :], kbuf.at[part, step], k_sem.at[part, step]
            ),
            pltpu.make_async_copy(
                sens_hbm.at[:, window, :], sbuf.at[part, step], s_sem.at[part, step]
            ),
        )

    block_copy.start()
    spat_copy.start()

    barrier = pltpu.get_barrier_semaphore()
    for shift in range(nf):
        for coil in range(nc):
            if shift or coil:
                pl.semaphore_signal(
                    barrier, inc=1,
                    device_id={"frame": xor(f, shift, nf), "coil": lax.rem(c + coil, nc)},
                    device_id_type=MESH,
                )

    def fetch(step):
        for part in range(nc):
            for copy in chunk_copies(step, part):
                copy.start()

    fetch(0)
    tslot[f] = jnp.concatenate(
        [
            temporal_ref[...].astype(F32),
            jnp.zeros((frames, LANES - 2 * rank), F32),
        ],
        -1,
    )

    pl.semaphore_wait(barrier, nf * nc - 1)
    for shift in range(1, nf):
        to = xor(f, shift, nf)
        remote(tslot.at[f], tslot.at[f], t_ssem.at[to], t_rsem.at[f], to, c).start()

    block_copy.wait()
    cosine, sine = block[:half, :half], block[:half, half:]
    transposed = jnp.concatenate(
        [jnp.concatenate([cosine, -sine], 1), jnp.concatenate([sine, cosine], 1)], 0
    )
    diagonal = iota((width, width), 0) == iota((width, width), 1)
    for t in range(frames):
        keep = sampled_ref[t : t + 1, :].astype(F32)
        keep = jnp.concatenate([keep, keep], -1)
        selector = jnp.where(diagonal, keep, 0.0).astype(BF)
        back[t] = mm(selector, transposed).astype(BF)

    spat_copy.wait()
    for shift in range(1, nf):
        source = xor(f, shift, nf)
        remote(
            tslot.at[source], tslot.at[source], t_ssem.at[source], t_rsem.at[source], source, c
        ).wait_recv()
    for source in range(nf):
        tall[source * frames : (source + 1) * frames] = tslot[source]
    long, deep = total_frames * rows, rows * rank
    repeat = one_hot(iota((long, total_frames), 0) // rows == iota((long, total_frames), 1))
    repeated = mm(repeat, tall[...].astype(BF)).astype(BF)
    lane, column = iota((LANES, deep), 0), iota((LANES, deep), 1)
    same_row = lax.rem(iota((long, deep), 0), rows) == iota((long, deep), 1) // rank
    spread_real = one_hot(lane == lax.rem(column, rank))
    spread_imag = one_hot(lane == lax.rem(column, rank) + rank)
    a_real = jnp.where(same_row, mm(repeated, spread_real), 0.0).astype(BF)
    a_imag = jnp.where(same_row, mm(repeated, spread_imag), 0.0).astype(BF)
    factors = spat[...].reshape(deep, width)
    by_real, by_imag = mm(a_real, factors), mm(a_imag, factors)
    image = jnp.concatenate(
        [by_real[:, :half] - by_imag[:, half:], by_real[:, half:] + by_imag[:, :half]], -1
    )
    for to in range(nf):
        for t in range(frames):
            at = (to * frames + t) * rows
            img_send[to, t] = image[at : at + rows].astype(BF)
    img_recv[0, f] = img_send[f]
    for shift in range(1, nf):
        shift = shift if nf < 3 else shift % (nf - 1) + 1
        to = xor(f, shift, nf)
        remote(
            img_send.at[to], img_recv.at[0, f], i_ssem.at[to], i_rsem.at[f], to, c
        ).start()

    for step in range(1, min(AHEAD, chunks)):
        fetch(step)

    row, lane = iota((deep, LANES), 0), iota((deep, LANES), 1)
    same_column = iota((deep, long), 0) // rank == lax.rem(iota((deep, long), 1), rows)
    from_real = one_hot(lane == lax.rem(row, rank))
    from_imag = one_hot(lane == lax.rem(row, rank) + rank)
    turn[:, :long] = jnp.where(same_column, mm_nt(from_real, repeated), 0.0).astype(BF)
    turn[:, long:] = jnp.where(same_column, mm_nt(from_imag, repeated), 0.0).astype(BF)
    turn_copy = pltpu.make_async_copy(turn, turn_hbm, turn_sem)
    turn_copy.start()

    def image_copy(source):
        return remote(
            img_send.at[source], img_recv.at[0, source], i_ssem.at[source], i_rsem.at[source],
            source, c,
        )

    def forward_copy(source):
        return remote(
            img_recv.at[0, source], img_recv.at[1, source], f_ssem.at[source],
            f_rsem.at[source], f, other,
        )

    def partial_copy(step):
        return remote(
            part_out.at[step], part_in.at[step], p_ssem.at[step], p_rsem.at[step], f, other
        )

    def gradient(step, part):
        where = chunk_at(step)
        for i in range(pieces):
            for t in range(frames):
                img_f32[t, i * rows : (i + 1) * rows] = img_recv[
                    part, where * pieces + i, t
                ].astype(F32)
        for copy in chunk_copies(step, part):
            copy.wait()
        sums = []
        for t in range(frames):
            image_real, image_imag = img_f32[t, :, :half], img_f32[t, :, half:]
            sens = sbuf[part, step].astype(F32)
            sens_real, sens_imag = sens[..., :half], sens[..., half:]
            coil_image = jnp.concatenate(
                [
                    sens_real * image_real[None] - sens_imag * image_imag[None],
                    sens_real * image_imag[None] + sens_imag * image_real[None],
                ],
                -1,
            ).astype(BF)
            spectrum = mm(coil_image.reshape(coils * chunk, width), block[...])
            measured = kbuf[part, step, t].reshape(coils * chunk, width).astype(F32)
            misfit = (spectrum - measured).astype(BF)
            adjoint = mm(misfit, back[t]).reshape(coils, chunk, width)
            back_real, back_imag = adjoint[..., :half], adjoint[..., half:]
            sums.append(
                jnp.concatenate(
                    [
                        jnp.sum(sens_real * back_real + sens_imag * back_imag, axis=0),
                        jnp.sum(sens_real * back_imag - sens_imag * back_real, axis=0),
                    ],
                    -1,
                )
            )
        return sums

    def finish(step):
        where = chunk_at(step)
        partial_copy(step).wait_recv()
        for t in range(frames):
            total = part_own[step, t] + part_in[step, t]
            for i in range(pieces):
                g_send[where * pieces + i, t] = total[i * rows : (i + 1) * rows].astype(BF)
        for i in range(pieces):
            to = where * pieces + i

            @pl.when(to != f)
            def _():
                remote(
                    g_send.at[to], g_recv.at[f], g_ssem.at[to], g_rsem.at[f], to, c
                ).start()

            @pl.when(to == f)
            def _():
                g_recv[f] = g_send[f]

    @pl.loop(0, chunks)
    def _(step):
        @pl.when(step + AHEAD < chunks)
        def _():
            fetch(step + AHEAD)

        where = chunk_at(step)
        for i in range(pieces):
            source = where * pieces + i

            @pl.when(source != f)
            def _():
                image_copy(source).wait_recv()

            forward_copy(source).start()
        for t, value in enumerate(gradient(step, 0)):
            part_own[step, t] = value

        @pl.when(step > 0)
        def _():
            finish(step - 1)

        for i in range(pieces):
            forward_copy(where * pieces + i).wait_recv()
        for t, value in enumerate(gradient(step, 1)):
            part_out[step, t] = value
        partial_copy(step).start()

    finish(chunks - 1)

    def gradient_copy(source):
        return remote(
            g_send.at[source], g_recv.at[source], g_ssem.at[source], g_rsem.at[source], source, c
        )

    for shift in range(1, nf):
        gradient_copy(xor(f, shift, nf)).wait_recv()
    for source in range(nf):
        for t in range(frames):
            at = (source * frames + t) * rows
            g_full[at : at + rows] = g_recv[source, t].astype(F32)
    grad = g_full[...].astype(BF)
    turned = jnp.concatenate([grad[:, half:], -grad[:, :half]], -1)
    grad_rows[:long] = grad
    grad_rows[long:] = turned
    grad_copy = pltpu.make_async_copy(grad_rows, grad_hbm, grad_sem)
    grad_copy.start()
    factors = spat[...].reshape(deep, width)
    fold_row, fold_lane = iota((deep, LANES), 0), iota((deep, LANES), 1)
    pooled = jnp.zeros((long, LANES), F32)
    for values, shift in ((grad, 0), (turned, rank)):
        products = jnp.where(same_row, mm_nt(values, factors), 0.0)
        fold = one_hot(lax.rem(fold_row, rank) + shift == fold_lane)
        high = products.astype(BF)
        low = (products - high.astype(F32)).astype(BF)
        pooled = pooled + mm(high, fold) + mm(low, fold)
    gather = one_hot(iota((total_frames, long), 0) == iota((total_frames, long), 1) // rows)
    high = pooled.astype(BF)
    low = (pooled - high.astype(F32)).astype(BF)
    temporal_part = mm(gather, high) + mm(gather, low)
    for to in range(nf):
        tg_send[to] = temporal_part[to * frames : (to + 1) * frames]
    tg_recv[c, f] = tg_send[f]
    for shift in range(nf):
        for coil in range(nc):
            if shift or coil:
                to, at = xor(f, shift, nf), lax.rem(c + coil, nc)
                remote(
                    tg_send.at[to], tg_recv.at[c, f], tg_ssem.at[at, to], tg_rsem.at[c, f], to, at
                ).start()

    for shift in range(nf):
        for coil in range(nc):
            if shift or coil:
                to, at = xor(f, shift, nf), lax.rem(c + coil, nc)
                remote(
                    tg_send.at[to], tg_recv.at[at, to], tg_ssem.at[at, to], tg_rsem.at[at, to],
                    to, at,
                ).wait()
    summed = tg_recv[0, 0]
    for coil in range(nc):
        for source in range(nf):
            if coil or source:
                summed = summed + tg_recv[coil, source]
    tgrad_ref[...] = summed[:, : 2 * rank]

    for shift in range(nf):
        to = xor(f, shift, nf)
        forward_copy(to).wait_send()
        if shift:
            remote(tslot.at[f], tslot.at[f], t_ssem.at[to], t_rsem.at[f], to, c).wait_send()
            image_copy(to).wait_send()
            gradient_copy(to).wait_send()

    @pl.loop(0, chunks)
    def _(step):
        partial_copy(step).wait_send()

    turn_copy.wait()
    grad_copy.wait()


def factor_kernel(turn_ref, grad_ref, tsum_ref, out_ref, tgrad_ref):
    out_ref[...] = mm(turn_ref[...], grad_ref[...]).reshape(out_ref.shape)
    tgrad_ref[...] = tsum_ref[...]


def on_device(nf, nc, spatial, temporal, kspace, sampled, sensitivity):
    rows, rank, width = spatial.shape
    frames, coils = kspace.shape[:2]
    chunk = max(rows, ROW_TILE)
    pieces = chunk // rows
    chunks = nf // pieces
    total_frames = nf * frames
    long, deep = total_frames * rows, rows * rank
    dims = (nf, nc, frames, coils, rows, rank, width, chunk, pieces, chunks)
    vmem, dma = pltpu.VMEM, pltpu.SemaphoreType.DMA
    anywhere, inside = pl.BlockSpec(memory_space=pl.ANY), pl.BlockSpec(memory_space=pltpu.VMEM)
    turn, grad_rows, temporal_sum = pl.pallas_call(
        functools.partial(kernel, dims),
        out_shape=(
            jax.ShapeDtypeStruct((deep, 2 * long), BF),
            jax.ShapeDtypeStruct((2 * long, width), BF),
            jax.ShapeDtypeStruct(temporal.shape, F32),
        ),
        in_specs=[anywhere, inside, anywhere, inside, anywhere, anywhere],
        out_specs=(anywhere, anywhere, inside),
        scratch_shapes=[
            vmem((nc, chunks, frames, coils, chunk, width), BF),
            vmem((nc, chunks, coils, chunk, width), BF),
            vmem((rows, rank, width), BF),
            vmem((width, width), BF),
            vmem((frames, width, width), BF),
            vmem((nf, frames, LANES), F32),
            vmem((total_frames, LANES), F32),
            vmem((nf, frames, rows, width), BF),
            vmem((nc, nf, frames, rows, width), BF),
            vmem((frames, chunk, width), F32),
            vmem((deep, 2 * long), BF),
            vmem((chunks, frames, chunk, width), F32),
            vmem((chunks, frames, chunk, width), F32),
            vmem((chunks, frames, chunk, width), F32),
            vmem((nf, frames, rows, width), BF),
            vmem((nf, frames, rows, width), BF),
            vmem((long, width), F32),
            vmem((2 * long, width), BF),
            vmem((nf, frames, LANES), F32),
            vmem((nc, nf, frames, LANES), F32),
            dma((nc, chunks)),
            dma((nc, chunks)),
            dma,
            dma,
            dma,
            dma,
        ]
        + [dma((nf,))] * 6
        + [dma((chunks,))] * 2
        + [dma((nf,))] * 2
        + [dma((nc, nf))] * 2,
        compiler_params=pltpu.CompilerParams(
            collective_id=0, has_side_effects=True, vmem_limit_bytes=56 * 1024 * 1024
        ),
        cost_estimate=pl.CostEstimate(
            flops=8 * frames * coils * nc * chunks * chunk * width * width // 2,
            bytes_accessed=kspace.size * 2 + sensitivity.size * 2 + spatial.size * 6,
            transcendentals=0,
        ),
    )(spatial, temporal, kspace, sampled, sensitivity, jnp.asarray(dft_block(width // 2)))
    return pl.pallas_call(
        factor_kernel,
        out_shape=(
            jax.ShapeDtypeStruct(spatial.shape, F32),
            jax.ShapeDtypeStruct(temporal.shape, F32),
        ),
        in_specs=[inside] * 3,
        out_specs=(inside, inside),
        compiler_params=pltpu.CompilerParams(vmem_limit_bytes=24 * 1024 * 1024),
    )(turn, grad_rows, temporal_sum)


def solution(mesh):
    placed = (
        P(("cuts", "coil", "frame"), None, None),
        P(("cuts", "frame"), None),
        P(("cuts", "frame"), "coil", None, None),
        P(("cuts", "frame"), None),
        P(("cuts", "coil"), None, None),
    )
    return jax.shard_map(
        functools.partial(on_device, mesh.shape["frame"], mesh.shape["coil"]),
        mesh=mesh,
        in_specs=placed,
        out_specs=(P(("cuts", "coil", "frame"), None, None), P(("cuts", "frame"), None)),
        check_vma=False,
    )
```

```python
import functools
import math

import jax
import jax.numpy as jnp
import ml_dtypes
import numpy as np
from jax import lax
from jax.experimental import pallas as pl
from jax.experimental.pallas import tpu as pltpu
from jax.sharding import PartitionSpec as P

BF = jnp.bfloat16
F32 = jnp.float32
MESH = pl.DeviceIdType.MESH
ROW_TILE = 16
AHEAD = 3
LIMIT = 61 * 1024 * 1024
LANES = 128


def dft_block(length):
    index = np.arange(length, dtype=np.int64)
    angles = (index[:, None] * index[None, :] % length) * (2.0 * math.pi / length)
    norm_factor = 1.0 / math.sqrt(length)
    cosine = np.cos(angles) * norm_factor
    sine_part = -np.sin(angles) * norm_factor
    block = np.block([[cosine, sine_part], [-sine_part, cosine]])
    return block.astype(np.float32).astype(ml_dtypes.bfloat16)


def mm(a, b):
    return jnp.dot(a, b, preferred_element_type=F32)


def mm_nt(a, b):
    return lax.dot_general(a, b, (((1,), (1,)), ((), ())), preferred_element_type=F32)


def ring(a, b, count):
    total = a + b
    return jnp.where(total >= count, total - count, total)


def quotient(values, n):
    return values >> (n.bit_length() - 1) if n & (n - 1) == 0 else values // n


def remainder(values, n):
    return values & (n - 1) if n & (n - 1) == 0 else lax.rem(values, n)


def iota(shape, dim):
    return lax.broadcasted_iota(jnp.int32, shape, dim)


def one_hot(condition):
    return jnp.where(condition, 1.0, 0.0).astype(BF)


def kernel(
    dims,
    spatial_hbm, temporal_ref, kspace_hbm, sampled_ref, sens_hbm, block_hbm,
    turn_hbm, grad_hbm, tgrad_ref,
    kbuf, sbuf, spat, block, back, tslot, tall, img_send, img_recv, img_f32,
    turn, part_own, part_out, part_in, g_send, g_recv, g_full,
    grad_rows, tg_send, tg_recv,
    k_sem, s_sem, spat_sem, block_sem, turn_sem, grad_sem,
    t_ssem, t_rsem, i_ssem, i_rsem, f_ssem, f_rsem, p_ssem, p_rsem,
    g_ssem, g_rsem, tg_ssem, tg_rsem,
):
    nf, nc, frames, coils, rows, rank, width, chunk, pieces, chunks = dims
    half = width // 2
    total_frames = nf * frames
    f, c = lax.axis_index("frame"), lax.axis_index("coil")
    other = nc - 1 - c
    mine = f if pieces == 1 else f // pieces

    def chunk_at(step):
        return ring(mine, step, chunks)

    def remote(src, dst, ssem, rsem, frame, coil):
        return pltpu.make_async_remote_copy(
            src_ref=src, dst_ref=dst, send_sem=ssem, recv_sem=rsem,
            device_id={"frame": frame, "coil": coil}, device_id_type=MESH,
        )

    spat_copy = pltpu.make_async_copy(spatial_hbm, spat, spat_sem)
    block_copy = pltpu.make_async_copy(block_hbm, block, block_sem)

    def chunk_copies(step, part):
        owner = c if part == 0 else other
        start = pl.multiple_of((owner * chunks + chunk_at(step)) * chunk, chunk)
        window = pl.ds(start, chunk)
        return (
            pltpu.make_async_copy(
                kspace_hbm.at[:, :, window, :], kbuf.at[part, step], k_sem.at[part, step]
            ),
            pltpu.make_async_copy(
                sens_hbm.at[:, window, :], sbuf.at[part, step], s_sem.at[part, step]
            ),
        )

    block_copy.start()
    spat_copy.start()

    barrier = pltpu.get_barrier_semaphore()
    for shift in range(nf):
        for coil in range(nc):
            if shift or coil:
                pl.semaphore_signal(
                    barrier, inc=1,
                    device_id={"frame": ring(f, shift, nf), "coil": (other if coil else c)},
                    device_id_type=MESH,
                )

    def fetch(step):
        for part in range(nc):
            for copy in chunk_copies(step, part):
                copy.start()

    fetch(0)
    tslot[f] = jnp.concatenate(
        [
            temporal_ref[...].astype(F32),
            jnp.zeros((frames, LANES - 2 * rank), F32),
        ],
        -1,
    )

    pl.semaphore_wait(barrier, nf * nc - 1)
    for shift in range(1, nf):
        to = ring(f, shift, nf)
        remote(tslot.at[f], tslot.at[f], t_ssem.at[to], t_rsem.at[f], to, c).start()

    block_copy.wait()
    cosine, sine = block[:half, :half], block[:half, half:]
    transposed = jnp.concatenate(
        [jnp.concatenate([cosine, -sine], 1), jnp.concatenate([sine, cosine], 1)], 0
    )
    diagonal = iota((width, width), 0) == iota((width, width), 1)
    for t in range(frames):
        keep = sampled_ref[t : t + 1, :].astype(F32)
        keep = jnp.concatenate([keep, keep], -1)
        selector = jnp.where(diagonal, keep, 0.0).astype(BF)
        back[t] = mm(selector, transposed).astype(BF)

    spat_copy.wait()
    for shift in range(1, nf):
        source = ring(f, shift, nf)
        remote(
            tslot.at[source], tslot.at[source], t_ssem.at[source], t_rsem.at[source], source, c
        ).wait_recv()
    for source in range(nf):
        tall[source * frames : (source + 1) * frames] = tslot[source]
    long, deep = total_frames * rows, rows * rank
    repeat = one_hot(quotient(iota((long, total_frames), 0), rows) == iota((long, total_frames), 1))
    repeated = mm(repeat, tall[...].astype(BF)).astype(BF)
    lane, column = iota((LANES, deep), 0), iota((LANES, deep), 1)
    same_row = remainder(iota((long, deep), 0), rows) == quotient(iota((long, deep), 1), rank)
    spread_real = one_hot(lane == remainder(column, rank))
    spread_imag = one_hot(lane == remainder(column, rank) + rank)
    a_real = jnp.where(same_row, mm(repeated, spread_real), 0.0).astype(BF)
    a_imag = jnp.where(same_row, mm(repeated, spread_imag), 0.0).astype(BF)
    factors = spat[...].reshape(deep, width)
    by_real, by_imag = mm(a_real, factors), mm(a_imag, factors)
    image = jnp.concatenate(
        [by_real[:, :half] - by_imag[:, half:], by_real[:, half:] + by_imag[:, :half]], -1
    )
    for to in range(nf):
        for t in range(frames):
            at = (to * frames + t) * rows
            img_send[to, t] = image[at : at + rows].astype(BF)
    img_recv[0, f] = img_send[f]
    for shift in range(1, nf):
        to = ring(f, shift, nf)
        remote(
            img_send.at[to], img_recv.at[0, f], i_ssem.at[to], i_rsem.at[f], to, c
        ).start()

    for step in range(1, min(AHEAD, chunks)):
        fetch(step)

    row, lane = iota((deep, LANES), 0), iota((deep, LANES), 1)
    same_column = quotient(iota((deep, long), 0), rank) == remainder(iota((deep, long), 1), rows)
    from_real = one_hot(lane == remainder(row, rank))
    from_imag = one_hot(lane == remainder(row, rank) + rank)
    turn[:, :long] = jnp.where(same_column, mm_nt(from_real, repeated), 0.0).astype(BF)
    turn[:, long:] = jnp.where(same_column, mm_nt(from_imag, repeated), 0.0).astype(BF)
    turn_copy = pltpu.make_async_copy(turn, turn_hbm, turn_sem)
    turn_copy.start()

    def image_copy(source):
        return remote(
            img_send.at[source], img_recv.at[0, source], i_ssem.at[source], i_rsem.at[source],
            source, c,
        )

    def forward_copy(source):
        return remote(
            img_recv.at[0, source], img_recv.at[1, source], f_ssem.at[source],
            f_rsem.at[source], f, other,
        )

    def partial_copy(step):
        return remote(
            part_out.at[step], part_in.at[step], p_ssem.at[step], p_rsem.at[step], f, other
        )

    def gradient(step, part):
        where = chunk_at(step)
        for i in range(pieces):
            for t in range(frames):
                img_f32[t, i * rows : (i + 1) * rows] = img_recv[
                    part, where * pieces + i, t
                ].astype(F32)
        for copy in chunk_copies(step, part):
            copy.wait()
        sums = []
        for t in range(frames):
            image_real, image_imag = img_f32[t, :, :half], img_f32[t, :, half:]
            sens = sbuf[part, step].astype(F32)
            sens_real, sens_imag = sens[..., :half], sens[..., half:]
            coil_image = jnp.concatenate(
                [
                    sens_real * image_real[None] - sens_imag * image_imag[None],
                    sens_real * image_imag[None] + sens_imag * image_real[None],
                ],
                -1,
            ).astype(BF)
            spectrum = mm(coil_image.reshape(coils * chunk, width), block[...])
            measured = kbuf[part, step, t].reshape(coils * chunk, width).astype(F32)
            misfit = (spectrum - measured).astype(BF)
            adjoint = mm(misfit, back[t]).reshape(coils, chunk, width)
            back_real, back_imag = adjoint[..., :half], adjoint[..., half:]
            sums.append(
                jnp.concatenate(
                    [
                        jnp.sum(sens_real * back_real + sens_imag * back_imag, axis=0),
                        jnp.sum(sens_real * back_imag - sens_imag * back_real, axis=0),
                    ],
                    -1,
                )
            )
        return sums

    def finish(step):
        where = chunk_at(step)
        partial_copy(step).wait_recv()
        for t in range(frames):
            total = part_own[step, t] + part_in[step, t]
            for i in range(pieces):
                g_send[where * pieces + i, t] = total[i * rows : (i + 1) * rows].astype(BF)
        for i in range(pieces):
            to = where * pieces + i

            @pl.when(to != f)
            def _():
                remote(
                    g_send.at[to], g_recv.at[f], g_ssem.at[to], g_rsem.at[f], to, c
                ).start()

            @pl.when(to == f)
            def _():
                g_recv[f] = g_send[f]

    @pl.loop(0, chunks)
    def _(step):
        @pl.when(step + AHEAD < chunks)
        def _():
            fetch(step + AHEAD)

        where = chunk_at(step)
        for i in range(pieces):
            source = where * pieces + i

            @pl.when(source != f)
            def _():
                image_copy(source).wait_recv()

            forward_copy(source).start()
        for t, value in enumerate(gradient(step, 0)):
            part_own[step, t] = value

        @pl.when(step > 0)
        def _():
            finish(step - 1)

        for i in range(pieces):
            forward_copy(where * pieces + i).wait_recv()
        for t, value in enumerate(gradient(step, 1)):
            part_out[step, t] = value
        partial_copy(step).start()

    finish(chunks - 1)

    def gradient_copy(source):
        return remote(
            g_send.at[source], g_recv.at[source], g_ssem.at[source], g_rsem.at[source], source, c
        )

    for shift in range(1, nf):
        gradient_copy(ring(f, shift, nf)).wait_recv()
    for source in range(nf):
        for t in range(frames):
            at = (source * frames + t) * rows
            g_full[at : at + rows] = g_recv[source, t].astype(F32)
    grad = g_full[...].astype(BF)
    turned = jnp.concatenate([grad[:, half:], -grad[:, :half]], -1)
    grad_rows[:long] = grad
    grad_rows[long:] = turned
    grad_copy = pltpu.make_async_copy(grad_rows, grad_hbm, grad_sem)
    grad_copy.start()
    factors = spat[...].reshape(deep, width)
    fold_row, fold_lane = iota((deep, LANES), 0), iota((deep, LANES), 1)
    pooled = jnp.zeros((long, LANES), F32)
    for values, shift in ((grad, 0), (turned, rank)):
        products = jnp.where(same_row, mm_nt(values, factors), 0.0)
        fold = one_hot(remainder(fold_row, rank) + shift == fold_lane)
        high = products.astype(BF)
        low = (products - high.astype(F32)).astype(BF)
        pooled = pooled + mm(high, fold) + mm(low, fold)
    gather = one_hot(iota((total_frames, long), 0) == quotient(iota((total_frames, long), 1), rows))
    high = pooled.astype(BF)
    low = (pooled - high.astype(F32)).astype(BF)
    temporal_part = mm(gather, high) + mm(gather, low)
    for to in range(nf):
        tg_send[to] = temporal_part[to * frames : (to + 1) * frames]
    tg_recv[c, f] = tg_send[f]
    for shift in range(nf):
        for coil in range(nc):
            if shift or coil:
                to, at = ring(f, shift, nf), (other if coil else c)
                remote(
                    tg_send.at[to], tg_recv.at[c, f], tg_ssem.at[at, to], tg_rsem.at[c, f], to, at
                ).start()

    for shift in range(nf):
        for coil in range(nc):
            if shift or coil:
                to, at = ring(f, shift, nf), (other if coil else c)
                remote(
                    tg_send.at[to], tg_recv.at[at, to], tg_ssem.at[at, to], tg_rsem.at[at, to],
                    to, at,
                ).wait()
    summed = tg_recv[0, 0]
    for coil in range(nc):
        for source in range(nf):
            if coil or source:
                summed = summed + tg_recv[coil, source]
    tgrad_ref[...] = summed[:, : 2 * rank]

    for shift in range(nf):
        to = ring(f, shift, nf)
        forward_copy(to).wait_send()
        if shift:
            remote(tslot.at[f], tslot.at[f], t_ssem.at[to], t_rsem.at[f], to, c).wait_send()
            image_copy(to).wait_send()
            gradient_copy(to).wait_send()

    @pl.loop(0, chunks)
    def _(step):
        partial_copy(step).wait_send()

    turn_copy.wait()
    grad_copy.wait()


def factor_kernel(
    turn_hbm, grad_hbm, tsum_hbm, out_ref, tgrad_ref, turn, grad_rows, turn_sem, grad_sem, tsum_sem
):
    copies = (
        pltpu.make_async_copy(turn_hbm, turn, turn_sem),
        pltpu.make_async_copy(grad_hbm, grad_rows, grad_sem),
        pltpu.make_async_copy(tsum_hbm, tgrad_ref, tsum_sem),
    )
    for copy in copies:
        copy.start()
    for copy in copies:
        copy.wait()
    out_ref[...] = mm(turn[...], grad_rows[...]).reshape(out_ref.shape)


def on_device(nf, nc, spatial, temporal, kspace, sampled, sensitivity):
    rows, rank, width = spatial.shape
    frames, coils = kspace.shape[:2]
    chunk = max(rows, ROW_TILE)
    pieces = chunk // rows
    chunks = nf // pieces
    total_frames = nf * frames
    long, deep = total_frames * rows, rows * rank
    dims = (nf, nc, frames, coils, rows, rank, width, chunk, pieces, chunks)
    vmem, dma = pltpu.VMEM, pltpu.SemaphoreType.DMA
    anywhere, inside = pl.BlockSpec(memory_space=pl.ANY), pl.BlockSpec(memory_space=pltpu.VMEM)
    turn, grad_rows, temporal_sum = pl.pallas_call(
        functools.partial(kernel, dims),
        out_shape=(
            jax.ShapeDtypeStruct((deep, 2 * long), BF),
            jax.ShapeDtypeStruct((2 * long, width), BF),
            jax.ShapeDtypeStruct(temporal.shape, F32),
        ),
        in_specs=[anywhere, inside, anywhere, inside, anywhere, anywhere],
        out_specs=(anywhere, anywhere, inside),
        scratch_shapes=[
            vmem((nc, chunks, frames, coils, chunk, width), BF),
            vmem((nc, chunks, coils, chunk, width), BF),
            vmem((rows, rank, width), BF),
            vmem((width, width), BF),
            vmem((frames, width, width), BF),
            vmem((nf, frames, LANES), F32),
            vmem((total_frames, LANES), F32),
            vmem((nf, frames, rows, width), BF),
            vmem((nc, nf, frames, rows, width), BF),
            vmem((frames, chunk, width), F32),
            vmem((deep, 2 * long), BF),
            vmem((chunks, frames, chunk, width), F32),
            vmem((chunks, frames, chunk, width), F32),
            vmem((chunks, frames, chunk, width), F32),
            vmem((nf, frames, rows, width), BF),
            vmem((nf, frames, rows, width), BF),
            vmem((long, width), F32),
            vmem((2 * long, width), BF),
            vmem((nf, frames, LANES), F32),
            vmem((nc, nf, frames, LANES), F32),
            dma((nc, chunks)),
            dma((nc, chunks)),
            dma,
            dma,
            dma,
            dma,
        ]
        + [dma((nf,))] * 6
        + [dma((chunks,))] * 2
        + [dma((nf,))] * 2
        + [dma((nc, nf))] * 2,
        compiler_params=pltpu.CompilerParams(
            collective_id=0, has_side_effects=True, vmem_limit_bytes=LIMIT
        ),
        cost_estimate=pl.CostEstimate(
            flops=8 * frames * coils * nc * chunks * chunk * width * width // 2,
            bytes_accessed=kspace.size * 2 + sensitivity.size * 2 + spatial.size * 6,
            transcendentals=0,
        ),
    )(spatial, temporal, kspace, sampled, sensitivity, jnp.asarray(dft_block(width // 2)))
    return pl.pallas_call(
        factor_kernel,
        out_shape=(
            jax.ShapeDtypeStruct(spatial.shape, F32),
            jax.ShapeDtypeStruct(temporal.shape, F32),
        ),
        in_specs=[anywhere] * 3,
        out_specs=(inside, inside),
        scratch_shapes=[vmem(turn.shape, BF), vmem(grad_rows.shape, BF), dma, dma, dma],
        compiler_params=pltpu.CompilerParams(vmem_limit_bytes=LIMIT),
    )(turn, grad_rows, temporal_sum)


def solution(mesh):
    placed = (
        P(("cuts", "coil", "frame"), None, None),
        P(("cuts", "frame"), None),
        P(("cuts", "frame"), "coil", None, None),
        P(("cuts", "frame"), None),
        P(("cuts", "coil"), None, None),
    )
    return jax.shard_map(
        functools.partial(on_device, mesh.shape["frame"], mesh.shape["coil"]),
        mesh=mesh,
        in_specs=placed,
        out_specs=(P(("cuts", "coil", "frame"), None, None), P(("cuts", "frame"), None)),
        check_vma=False,
    )
```

```python
import functools
import math

import jax
import jax.numpy as jnp
import ml_dtypes
import numpy as np
from jax import lax
from jax.experimental import pallas as pl
from jax.experimental.pallas import tpu as pltpu
from jax.sharding import PartitionSpec as P

BF = jnp.bfloat16
F32 = jnp.float32
MESH = pl.DeviceIdType.MESH
ROW_TILE = 16
AHEAD = 3
LIMIT = 61 * 1024 * 1024
LANES = 128


def dft_block(length):
    index = np.arange(length, dtype=np.int64)
    angles = (index[:, None] * index[None, :] % length) * (2.0 * math.pi / length)
    norm_factor = 1.0 / math.sqrt(length)
    cosine = np.cos(angles) * norm_factor
    sine_part = -np.sin(angles) * norm_factor
    block = np.block([[cosine, sine_part], [-sine_part, cosine]])
    return block.astype(np.float32).astype(ml_dtypes.bfloat16)


def mm(a, b):
    return jnp.dot(a, b, preferred_element_type=F32)


def mm_nt(a, b):
    return lax.dot_general(a, b, (((1,), (1,)), ((), ())), preferred_element_type=F32)


def xor(a, b, count):
    if count & (count - 1):
        return lax.rem(a + b, count)
    total, bit = 0, 1
    while bit < count:
        if isinstance(b, int):
            digit = lax.rem(lax.div(a, bit), 2)
            total = total + bit * ((1 - digit) if b & bit else digit)
        else:
            total = total + bit * lax.rem(lax.div(a, bit) + lax.div(b, bit), 2)
        bit *= 2
    return total


def quotient(values, n):
    return values >> (n.bit_length() - 1) if n & (n - 1) == 0 else values // n


def remainder(values, n):
    return values & (n - 1) if n & (n - 1) == 0 else lax.rem(values, n)


def iota(shape, dim):
    return lax.broadcasted_iota(jnp.int32, shape, dim)


def one_hot(condition):
    return jnp.where(condition, 1.0, 0.0).astype(BF)


def kernel(
    dims,
    spatial_hbm, temporal_ref, kspace_hbm, sampled_ref, sens_hbm, block_hbm,
    turn_hbm, grad_hbm, tgrad_ref,
    kbuf, sbuf, spat, block, back, tslot, tall, img_send, img_recv, img_f32,
    turn, part_own, part_out, part_in, g_send, g_recv, g_full,
    grad_rows, tg_send, tg_recv,
    k_sem, s_sem, spat_sem, block_sem, turn_sem, grad_sem,
    t_ssem, t_rsem, i_ssem, i_rsem, f_ssem, f_rsem, p_ssem, p_rsem,
    g_ssem, g_rsem, tg_ssem, tg_rsem,
):
    nf, nc, frames, coils, rows, rank, width, chunk, pieces, chunks = dims
    half = width // 2
    total_frames = nf * frames
    f, c = lax.axis_index("frame"), lax.axis_index("coil")
    other = nc - 1 - c
    mine = f if pieces == 1 else f // pieces

    def order(step):
        if chunks < 3:
            return step
        if isinstance(step, int):
            return step % (chunks - 1) + 1 if step else 0
        later = lax.div(step + chunks - 1, chunks)
        return (lax.rem(step, chunks - 1) + 1) * later

    def chunk_at(step):
        return xor(mine, order(step), chunks)

    def remote(src, dst, ssem, rsem, frame, coil):
        return pltpu.make_async_remote_copy(
            src_ref=src, dst_ref=dst, send_sem=ssem, recv_sem=rsem,
            device_id={"frame": frame, "coil": coil}, device_id_type=MESH,
        )

    spat_copy = pltpu.make_async_copy(spatial_hbm, spat, spat_sem)
    block_copy = pltpu.make_async_copy(block_hbm, block, block_sem)

    def chunk_copies(step, part):
        owner = c if part == 0 else other
        start = pl.multiple_of((owner * chunks + chunk_at(step)) * chunk, chunk)
        window = pl.ds(start, chunk)
        return (
            pltpu.make_async_copy(
                kspace_hbm.at[:, :, window, :], kbuf.at[part, step], k_sem.at[part, step]
            ),
            pltpu.make_async_copy(
                sens_hbm.at[:, window, :], sbuf.at[part, step], s_sem.at[part, step]
            ),
        )

    block_copy.start()
    spat_copy.start()

    barrier = pltpu.get_barrier_semaphore()
    for shift in range(nf):
        for coil in range(nc):
            if shift or coil:
                pl.semaphore_signal(
                    barrier, inc=1,
                    device_id={"frame": xor(f, shift, nf), "coil": (other if coil else c)},
                    device_id_type=MESH,
                )

    def fetch(step):
        for part in range(nc):
            for copy in chunk_copies(step, part):
                copy.start()

    fetch(0)
    tslot[f] = jnp.concatenate(
        [
            temporal_ref[...].astype(F32),
            jnp.zeros((frames, LANES - 2 * rank), F32),
        ],
        -1,
    )

    pl.semaphore_wait(barrier, nf * nc - 1)
    for shift in range(1, nf):
        to = xor(f, shift, nf)
        remote(tslot.at[f], tslot.at[f], t_ssem.at[to], t_rsem.at[f], to, c).start()

    block_copy.wait()
    cosine, sine = block[:half, :half], block[:half, half:]
    transposed = jnp.concatenate(
        [jnp.concatenate([cosine, -sine], 1), jnp.concatenate([sine, cosine], 1)], 0
    )
    diagonal = iota((width, width), 0) == iota((width, width), 1)
    for t in range(frames):
        keep = sampled_ref[t : t + 1, :].astype(F32)
        keep = jnp.concatenate([keep, keep], -1)
        selector = jnp.where(diagonal, keep, 0.0).astype(BF)
        back[t] = mm(selector, transposed).astype(BF)

    spat_copy.wait()
    for shift in range(1, nf):
        source = xor(f, shift, nf)
        remote(
            tslot.at[source], tslot.at[source], t_ssem.at[source], t_rsem.at[source], source, c
        ).wait_recv()
    for source in range(nf):
        tall[source * frames : (source + 1) * frames] = tslot[source]
    long, deep = total_frames * rows, rows * rank
    repeat = one_hot(quotient(iota((long, total_frames), 0), rows) == iota((long, total_frames), 1))
    repeated = mm(repeat, tall[...].astype(BF)).astype(BF)
    lane, column = iota((LANES, deep), 0), iota((LANES, deep), 1)
    same_row = remainder(iota((long, deep), 0), rows) == quotient(iota((long, deep), 1), rank)
    spread_real = one_hot(lane == remainder(column, rank))
    spread_imag = one_hot(lane == remainder(column, rank) + rank)
    a_real = jnp.where(same_row, mm(repeated, spread_real), 0.0).astype(BF)
    a_imag = jnp.where(same_row, mm(repeated, spread_imag), 0.0).astype(BF)
    factors = spat[...].reshape(deep, width)
    by_real, by_imag = mm(a_real, factors), mm(a_imag, factors)
    image = jnp.concatenate(
        [by_real[:, :half] - by_imag[:, half:], by_real[:, half:] + by_imag[:, :half]], -1
    )
    for to in range(nf):
        for t in range(frames):
            at = (to * frames + t) * rows
            img_send[to, t] = image[at : at + rows].astype(BF)
    img_recv[0, f] = img_send[f]
    for shift in range(1, nf):
        shift = shift if nf < 3 else shift % (nf - 1) + 1
        to = xor(f, shift, nf)
        remote(
            img_send.at[to], img_recv.at[0, f], i_ssem.at[to], i_rsem.at[f], to, c
        ).start()

    for step in range(1, min(AHEAD, chunks)):
        fetch(step)

    row, lane = iota((deep, LANES), 0), iota((deep, LANES), 1)
    same_column = quotient(iota((deep, long), 0), rank) == remainder(iota((deep, long), 1), rows)
    from_real = one_hot(lane == remainder(row, rank))
    from_imag = one_hot(lane == remainder(row, rank) + rank)
    turn[:, :long] = jnp.where(same_column, mm_nt(from_real, repeated), 0.0).astype(BF)
    turn[:, long:] = jnp.where(same_column, mm_nt(from_imag, repeated), 0.0).astype(BF)
    turn_copy = pltpu.make_async_copy(turn, turn_hbm, turn_sem)
    turn_copy.start()

    def image_copy(source):
        return remote(
            img_send.at[source], img_recv.at[0, source], i_ssem.at[source], i_rsem.at[source],
            source, c,
        )

    def forward_copy(source):
        return remote(
            img_recv.at[0, source], img_recv.at[1, source], f_ssem.at[source],
            f_rsem.at[source], f, other,
        )

    def partial_copy(step):
        return remote(
            part_out.at[step], part_in.at[step], p_ssem.at[step], p_rsem.at[step], f, other
        )

    def gradient(step, part):
        where = chunk_at(step)
        if pieces > 1:
            for i in range(pieces):
                for t in range(frames):
                    img_f32[t, i * rows : (i + 1) * rows] = img_recv[
                        part, where * pieces + i, t
                    ].astype(F32)
        for copy in chunk_copies(step, part):
            copy.wait()
        sums = []
        for t in range(frames):
            image = img_recv[part, where, t] if pieces == 1 else img_f32[t].astype(BF)
            image_real, image_imag = image[:, :half], image[:, half:]
            sens = sbuf[part, step]
            sens_real, sens_imag = sens[..., :half], sens[..., half:]
            coil_image = jnp.concatenate(
                [
                    sens_real * image_real[None] - sens_imag * image_imag[None],
                    sens_real * image_imag[None] + sens_imag * image_real[None],
                ],
                -1,
            )
            spectrum = mm(coil_image.reshape(coils * chunk, width), block[...])
            measured = kbuf[part, step, t].reshape(coils * chunk, width).astype(F32)
            misfit = (spectrum - measured).astype(BF)
            adjoint = mm(misfit, back[t]).reshape(coils, chunk, width)
            back_real, back_imag = adjoint[..., :half], adjoint[..., half:]
            sens_real, sens_imag = sens_real.astype(F32), sens_imag.astype(F32)
            sums.append(
                jnp.concatenate(
                    [
                        jnp.sum(sens_real * back_real + sens_imag * back_imag, axis=0),
                        jnp.sum(sens_real * back_imag - sens_imag * back_real, axis=0),
                    ],
                    -1,
                )
            )
        return sums

    def finish(step):
        where = chunk_at(step)
        partial_copy(step).wait_recv()
        for t in range(frames):
            total = part_own[step, t] + part_in[step, t]
            for i in range(pieces):
                g_send[where * pieces + i, t] = total[i * rows : (i + 1) * rows].astype(BF)
        for i in range(pieces):
            to = where * pieces + i

            @pl.when(to != f)
            def _():
                remote(
                    g_send.at[to], g_recv.at[f], g_ssem.at[to], g_rsem.at[f], to, c
                ).start()

            @pl.when(to == f)
            def _():
                g_recv[f] = g_send[f]

    @pl.loop(0, chunks)
    def _(step):
        @pl.when(step + AHEAD < chunks)
        def _():
            fetch(step + AHEAD)

        where = chunk_at(step)
        for i in range(pieces):
            source = where * pieces + i

            @pl.when(source != f)
            def _():
                image_copy(source).wait_recv()

            forward_copy(source).start()
        for t, value in enumerate(gradient(step, 0)):
            part_own[step, t] = value

        @pl.when(step > 0)
        def _():
            finish(step - 1)

        for i in range(pieces):
            forward_copy(where * pieces + i).wait_recv()
        for t, value in enumerate(gradient(step, 1)):
            part_out[step, t] = value
        partial_copy(step).start()

    finish(chunks - 1)

    def gradient_copy(source):
        return remote(
            g_send.at[source], g_recv.at[source], g_ssem.at[source], g_rsem.at[source], source, c
        )

    for shift in range(1, nf):
        gradient_copy(xor(f, shift, nf)).wait_recv()
    for source in range(nf):
        for t in range(frames):
            at = (source * frames + t) * rows
            g_full[at : at + rows] = g_recv[source, t].astype(F32)
    grad = g_full[...].astype(BF)
    turned = jnp.concatenate([grad[:, half:], -grad[:, :half]], -1)
    grad_rows[:long] = grad
    grad_rows[long:] = turned
    grad_copy = pltpu.make_async_copy(grad_rows, grad_hbm, grad_sem)
    grad_copy.start()
    factors = spat[...].reshape(deep, width)
    fold_row, fold_lane = iota((deep, LANES), 0), iota((deep, LANES), 1)
    pooled = jnp.zeros((long, LANES), F32)
    for values, shift in ((grad, 0), (turned, rank)):
        products = jnp.where(same_row, mm_nt(values, factors), 0.0)
        fold = one_hot(remainder(fold_row, rank) + shift == fold_lane)
        high = products.astype(BF)
        low = (products - high.astype(F32)).astype(BF)
        pooled = pooled + mm(high, fold) + mm(low, fold)
    gather = one_hot(iota((total_frames, long), 0) == quotient(iota((total_frames, long), 1), rows))
    high = pooled.astype(BF)
    low = (pooled - high.astype(F32)).astype(BF)
    temporal_part = mm(gather, high) + mm(gather, low)
    for to in range(nf):
        tg_send[to] = temporal_part[to * frames : (to + 1) * frames]
    tg_recv[c, f] = tg_send[f]
    for shift in range(nf):
        for coil in range(nc):
            if shift or coil:
                to, at = xor(f, shift, nf), (other if coil else c)
                remote(
                    tg_send.at[to], tg_recv.at[c, f], tg_ssem.at[at, to], tg_rsem.at[c, f], to, at
                ).start()

    for shift in range(nf):
        for coil in range(nc):
            if shift or coil:
                to, at = xor(f, shift, nf), (other if coil else c)
                remote(
                    tg_send.at[to], tg_recv.at[at, to], tg_ssem.at[at, to], tg_rsem.at[at, to],
                    to, at,
                ).wait()
    summed = tg_recv[0, 0]
    for coil in range(nc):
        for source in range(nf):
            if coil or source:
                summed = summed + tg_recv[coil, source]
    tgrad_ref[...] = summed[:, : 2 * rank]

    for shift in range(nf):
        to = xor(f, shift, nf)
        forward_copy(to).wait_send()
        if shift:
            remote(tslot.at[f], tslot.at[f], t_ssem.at[to], t_rsem.at[f], to, c).wait_send()
            image_copy(to).wait_send()
            gradient_copy(to).wait_send()

    @pl.loop(0, chunks)
    def _(step):
        partial_copy(step).wait_send()

    turn_copy.wait()
    grad_copy.wait()


def factor_kernel(
    turn_hbm, grad_hbm, tsum_hbm, out_ref, tgrad_ref, turn, grad_rows, turn_sem, grad_sem, tsum_sem
):
    copies = (
        pltpu.make_async_copy(turn_hbm, turn, turn_sem),
        pltpu.make_async_copy(grad_hbm, grad_rows, grad_sem),
        pltpu.make_async_copy(tsum_hbm, tgrad_ref, tsum_sem),
    )
    for copy in copies:
        copy.start()
    for copy in copies:
        copy.wait()
    out_ref[...] = mm(turn[...], grad_rows[...]).reshape(out_ref.shape)


def on_device(nf, nc, spatial, temporal, kspace, sampled, sensitivity):
    rows, rank, width = spatial.shape
    frames, coils = kspace.shape[:2]
    chunk = max(rows, ROW_TILE)
    pieces = chunk // rows
    chunks = nf // pieces
    total_frames = nf * frames
    long, deep = total_frames * rows, rows * rank
    dims = (nf, nc, frames, coils, rows, rank, width, chunk, pieces, chunks)
    vmem, dma = pltpu.VMEM, pltpu.SemaphoreType.DMA
    anywhere, inside = pl.BlockSpec(memory_space=pl.ANY), pl.BlockSpec(memory_space=pltpu.VMEM)
    turn, grad_rows, temporal_sum = pl.pallas_call(
        functools.partial(kernel, dims),
        out_shape=(
            jax.ShapeDtypeStruct((deep, 2 * long), BF),
            jax.ShapeDtypeStruct((2 * long, width), BF),
            jax.ShapeDtypeStruct(temporal.shape, F32),
        ),
        in_specs=[anywhere, inside, anywhere, inside, anywhere, anywhere],
        out_specs=(anywhere, anywhere, inside),
        scratch_shapes=[
            vmem((nc, chunks, frames, coils, chunk, width), BF),
            vmem((nc, chunks, coils, chunk, width), BF),
            vmem((rows, rank, width), BF),
            vmem((width, width), BF),
            vmem((frames, width, width), BF),
            vmem((nf, frames, LANES), F32),
            vmem((total_frames, LANES), F32),
            vmem((nf, frames, rows, width), BF),
            vmem((nc, nf, frames, rows, width), BF),
            vmem((frames, chunk, width), F32),
            vmem((deep, 2 * long), BF),
            vmem((chunks, frames, chunk, width), F32),
            vmem((chunks, frames, chunk, width), F32),
            vmem((chunks, frames, chunk, width), F32),
            vmem((nf, frames, rows, width), BF),
            vmem((nf, frames, rows, width), BF),
            vmem((long, width), F32),
            vmem((2 * long, width), BF),
            vmem((nf, frames, LANES), F32),
            vmem((nc, nf, frames, LANES), F32),
            dma((nc, chunks)),
            dma((nc, chunks)),
            dma,
            dma,
            dma,
            dma,
        ]
        + [dma((nf,))] * 6
        + [dma((chunks,))] * 2
        + [dma((nf,))] * 2
        + [dma((nc, nf))] * 2,
        compiler_params=pltpu.CompilerParams(
            collective_id=0, has_side_effects=True, vmem_limit_bytes=LIMIT
        ),
        cost_estimate=pl.CostEstimate(
            flops=8 * frames * coils * nc * chunks * chunk * width * width // 2,
            bytes_accessed=kspace.size * 2 + sensitivity.size * 2 + spatial.size * 6,
            transcendentals=0,
        ),
    )(spatial, temporal, kspace, sampled, sensitivity, jnp.asarray(dft_block(width // 2)))
    return pl.pallas_call(
        factor_kernel,
        out_shape=(
            jax.ShapeDtypeStruct(spatial.shape, F32),
            jax.ShapeDtypeStruct(temporal.shape, F32),
        ),
        in_specs=[anywhere] * 3,
        out_specs=(inside, inside),
        scratch_shapes=[vmem(turn.shape, BF), vmem(grad_rows.shape, BF), dma, dma, dma],
        compiler_params=pltpu.CompilerParams(vmem_limit_bytes=LIMIT),
    )(turn, grad_rows, temporal_sum)


def solution(mesh):
    placed = (
        P(("cuts", "coil", "frame"), None, None),
        P(("cuts", "frame"), None),
        P(("cuts", "frame"), "coil", None, None),
        P(("cuts", "frame"), None),
        P(("cuts", "coil"), None, None),
    )
    return jax.shard_map(
        functools.partial(on_device, mesh.shape["frame"], mesh.shape["coil"]),
        mesh=mesh,
        in_specs=placed,
        out_specs=(P(("cuts", "coil", "frame"), None, None), P(("cuts", "frame"), None)),
        check_vma=False,
    )
```
